32 devices in a mesh: dp: 16 (over z, y, core), tensor: 2 (over x).
Axes of the slice: x: 2, y: 2, z: 4, core: 2. Of those that a mesh axis runs over, the one named last changes fastest.
Arguments:
- resid_in: float32 [8192, 1024], P(('dp', 'tensor')), may hold values from -6 to 6
- segments: int32 [8192], P('dp'), may hold values from 0 to 15, never falling along the last dimension, each value on 1 to 1024 neighbouring positions
- cotangent: float32 [8192, 1024], P(('dp', 'tensor')), may hold values from -6 to 6
- norm_gain: float32 [2, 1024], replicated, may hold values from 0.25 to 1.75
- inner_proj: bfloat16 [2, 1024, 2, 2048], P(None, 'dp', None, 'tensor'), may hold values from -0.1875 to 0.1875
- shared_proj: bfloat16 [2, 1024, 288], replicated, may hold values from -0.1875 to 0.1875
- conv_weight: float32 [2, 4, 2304], replicated, may hold values from -3 to 3
- conv_bias: float32 [2, 2304], replicated, may hold values from -0.5 to 0.5
- dt_offset: float32 [2, 32], replicated, may hold values from -5 to -2
- rate_log: float32 [2, 32], replicated, may hold values from -2 to 2.5
- skip_gain: float32 [2, 32], replicated, may hold values from 0.5 to 1.5
- mix_gain: float32 [2, 2048], replicated, may hold values from 0.25 to 1.75
- out_proj: bfloat16 [2, 2048, 1024], P(None, 'tensor', 'dp'), may hold values from -0.125 to 0.125
Outputs:
- resid_out: float32 [8192, 1024], P(('dp', 'tensor'))
- grad_in: float32 [8192, 1024], P(('dp', 'tensor'))
- grad_norm_gain: float32 [2, 1024], replicated
- grad_inner_proj: float32 [2, 1024, 2, 2048], P(None, 'dp', None, 'tensor')
- grad_shared_proj: float32 [2, 1024, 288], replicated
- grad_conv_weight: float32 [2, 4, 2304], replicated
- grad_conv_bias: float32 [2, 2304], replicated
- grad_dt_offset: float32 [2, 32], replicated
- grad_rate_log: float32 [2, 32], replicated
- grad_skip_gain: float32 [2, 32], replicated
- grad_mix_gain: float32 [2, 2048], replicated
- grad_out_proj: float32 [2, 2048, 1024], P(None, 'tensor', 'dp')
The draws below stay inside these ranges and needn't reach their ends.
Inputs may be any that keep to these rules, and one draw needn't show every extreme that they name: `segments`: segment numbers never fall along the tokens; each segment covers 1 to 1024 consecutive tokens.
All inputs are finite; a program needn't handle non-finite values.
Results may differ from the reference program's by a relative error of at most 0.012.
Values may be sent and summed in bfloat16 or wider, within the bound.
A program may use at most 192 MiB of HBM per device.

```python
import math
import jax
import jax.numpy as jnp
import numpy as np
from jax import lax

D = 1024
HEADS = 32
HEADDIM = 64
STATE = 128
KCONV = 4
BLOCK = 256
LAYERS = 2
DOC_MAX = 1024
INNER = 2048
SEQ_LEN = 512
TOKENS = 8192
DOCS = 16


def level_of(rng, shape, split, smallest, largest):
    factor_of, own = 1.0, jax.random.fold_in(rng, 6)
    for dim, blocks in split:
        heights = jnp.exp(jax.random.uniform(jax.random.fold_in(own, dim), (blocks,), jnp.float32, smallest / len(split), largest / len(split)))
        factor_of = factor_of * jnp.repeat(heights, shape[dim] // blocks).reshape([-1 if axis == dim else 1 for axis in range(len(shape))])
    return factor_of


def split_up(count, total, limit, lean):
    portions = [(1 << 20) // math.isqrt(grade ** lean) + 1 for grade in range(2, count + 1)]
    surplus, holding = total - limit - (count - 1), [1] * (count - 1)
    while surplus > 0:
        free = [i for i in range(count - 1) if holding[i] < limit]
        mass, remaining = sum([portions[i] for i in free]), surplus
        for i in free:
            more = min(limit - holding[i], max(1, remaining * portions[i] // mass), surplus)
            holding[i] = holding[i] + more
            surplus = surplus - more
    return np.array([limit] + holding)


def uneven(stream_key, count, total, limit, skew):
    if count == 2:
        one = jax.random.randint(stream_key, (), max(1, total - limit), min(limit, total - 1) + 1)
        return jnp.stack([one, total - one])
    tallies = jnp.asarray(split_up(count, total, limit, skew), jnp.int32)
    twos = (count - 1) // 2
    giver, taker = tallies[1:1 + 2 * twos:2], tallies[2:2 + 2 * twos:2]
    slack = jnp.minimum(giver - 1, limit - taker)
    passed = jax.random.randint(jax.random.fold_in(stream_key, 1), (twos,), 0, 1 << 20) % (slack + 1)
    tallies = tallies.at[1:1 + 2 * twos:2].set(giver - passed).at[2:2 + 2 * twos:2].set(taker + passed)
    return tallies[jax.random.permutation(jax.random.fold_in(stream_key, 2), count)]


def gaussian(key, dims, scale, most, cuts=(), held_as=jnp.bfloat16):
    entries = scale * jax.random.normal(key, dims, jnp.float32)
    if cuts:
        entries = entries * level_of(key, dims, cuts, -0.22, 0.18)
    return jnp.clip(entries, -most, most).astype(held_as)


def setup_inputs(seed: int = 0) -> dict:
    key_of = jax.random.split(jax.random.key(seed), 14)
    return {
        "resid_in": gaussian(key_of[0], (TOKENS, D), 1.0, 6.0, ((0, 32),), jnp.float32),
        "segments": jnp.searchsorted(jnp.cumsum(uneven(key_of[1], DOCS, TOKENS, DOC_MAX, 0)), jnp.arange(TOKENS), side="right").astype(jnp.int32),
        "cotangent": gaussian(key_of[2], (TOKENS, D), 1.0, 6.0, ((0, 32),), jnp.float32),
        "norm_gain": jnp.clip(1.0 + 0.15 * jax.random.normal(key_of[3], (LAYERS, D), jnp.float32), 0.25, 1.75),
        "inner_proj": gaussian(key_of[4], (LAYERS, D, 2, INNER), D ** -0.5, 0.1875, ((1, 16), (3, 2))),
        "shared_proj": gaussian(key_of[5], (LAYERS, D, 2 * STATE + HEADS), D ** -0.5, 0.1875),
        "conv_weight": gaussian(key_of[6], (LAYERS, KCONV, INNER + 2 * STATE), KCONV ** -0.5, 3.0, (), jnp.float32),
        "conv_bias": jnp.clip(jax.random.uniform(key_of[7], (LAYERS, INNER + 2 * STATE), jnp.float32, -0.5, 0.5), -0.5, 0.5),
        "dt_offset": jnp.clip(jax.random.uniform(key_of[8], (LAYERS, HEADS), jnp.float32, -5.0, -2.0), -5.0, -2.0),
        "rate_log": jnp.clip(jax.random.uniform(key_of[9], (LAYERS, HEADS), jnp.float32, -2.0, 2.5), -2.0, 2.5),
        "skip_gain": jnp.clip(jax.random.uniform(key_of[10], (LAYERS, HEADS), jnp.float32, 0.5, 1.5), 0.5, 1.5),
        "mix_gain": jnp.clip(1.0 + 0.15 * jax.random.normal(key_of[11], (LAYERS, INNER), jnp.float32), 0.25, 1.75),
        "out_proj": gaussian(key_of[12], (LAYERS, INNER, D), INNER ** -0.5, 0.125, ((1, 2), (2, 16))),
    }


epsilon = 1e-05
precise = lax.Precision.HIGHEST

@jax.custom_vjp
def low(v):
    return lax.optimization_barrier(v.astype(jnp.bfloat16)).astype(jnp.float32)

@jax.custom_vjp
def low_back(v):
    return v

def low_keep(v):
    return (low(v), None)

def low_pass(kept, grad):
    return (grad,)

def back_keep(v):
    return (v, None)

def back_low(kept, grad):
    return (low(grad),)
low.defvjp(low_keep, low_pass)
low_back.defvjp(back_keep, back_low)

def causal_conv(values, weight, offset, segment):
    length = values.shape[0]
    tap_count = weight.shape[0]
    summed = offset[None, :] + weight[tap_count - 1][None, :] * values
    for lag_steps in range(1, tap_count):
        shifted = jnp.concatenate([jnp.zeros((lag_steps, values.shape[1]), values.dtype), values[:length - lag_steps]], axis=0)
        earlier = jnp.concatenate([jnp.full((lag_steps,), -1, jnp.int32), segment[:length - lag_steps]], axis=0)
        joined = (earlier == segment).astype(values.dtype)
        summed = summed + weight[tap_count - 1 - lag_steps][None, :] * shifted * joined[:, None]
    return summed

def state_space(x_heads, step_sizes, rates, b_rows, c_rows, segment, skip_gains):
    length, head_count, head_width = x_heads.shape
    blocks = length // BLOCK
    float_type = x_heads.dtype
    log_decay = -(step_sizes * rates[None, :])
    cumulative = jnp.transpose(jnp.cumsum(log_decay.reshape(blocks, BLOCK, head_count), axis=1), (0, 2, 1))
    step_blocks = jnp.transpose(step_sizes.reshape(blocks, BLOCK, head_count), (0, 2, 1))
    seg_blocks = segment.reshape(blocks, BLOCK)
    x_blocks = x_heads.reshape(blocks, BLOCK, head_count, head_width)
    b_blocks = b_rows.reshape(blocks, BLOCK, -1)
    c_blocks = c_rows.reshape(blocks, BLOCK, -1)
    positions = lax.iota(jnp.int32, BLOCK)
    causal = positions[:, None] >= positions[None, :]
    linked = (seg_blocks[:, :, None] == seg_blocks[:, None, :]) & causal[None]
    log_gap = cumulative[:, :, :, None] - cumulative[:, :, None, :]
    decays = jnp.exp(jnp.where(linked[:, None], log_gap, 0.0)) * linked[:, None].astype(float_type)
    pairing = jnp.einsum('kin,kjn->kij', c_blocks, b_blocks, precision=precise)
    mixing = pairing[:, None] * decays * step_blocks[:, :, None, :]
    inside = jnp.einsum('khij,kjhp->kihp', mixing, x_blocks, precision=precise)
    last_seg = seg_blocks[:, -1]
    same_end = (seg_blocks == last_seg[:, None]).astype(float_type)
    to_end = jnp.exp(cumulative[:, :, -1:] - cumulative) * same_end[:, None, :] * step_blocks
    weighted_x = x_blocks * jnp.transpose(to_end, (0, 2, 1))[:, :, :, None]
    block_states = jnp.einsum('kjn,kjhp->khnp', b_blocks, weighted_x, precision=precise)
    prior_seg = jnp.concatenate([jnp.full((1,), -1, jnp.int32), last_seg[:-1]])
    carry_on = (last_seg == prior_seg).astype(float_type)
    totals = jnp.exp(cumulative[:, :, -1])

    def advance(running, pieces):
        block_state, block_total, block_keep = pieces
        return (running * (block_total * block_keep)[:, None, None] + block_state, running)
    unused, entering = lax.scan(advance, jnp.zeros(block_states.shape[1:], float_type), (block_states, totals, carry_on))
    reaches = jnp.exp(cumulative) * (seg_blocks == prior_seg[:, None]).astype(float_type)[:, None, :]
    carried = jnp.einsum('kin,khnp->kihp', c_blocks, entering, precision=precise)
    carried = carried * jnp.transpose(reaches, (0, 2, 1))[:, :, :, None]
    result = inside + carried + skip_gains[None, None, :, None] * x_blocks
    return result.reshape(length, head_count * head_width)

def mixer_sequence(z_part, x_part, bc_raw, dt_raw, conv_x_weight, conv_x_offset, conv_bc_weight, conv_bc_offset, dt_shift, rate_logs, skip_gains, segment):
    length = x_part.shape[0]
    x_conv = jax.nn.silu(causal_conv(x_part, conv_x_weight, conv_x_offset, segment))
    bc_conv = jax.nn.silu(causal_conv(bc_raw, conv_bc_weight, conv_bc_offset, segment))
    step_sizes = jax.nn.softplus(dt_raw + dt_shift[None, :])
    rates = jnp.exp(rate_logs)
    mixed = state_space(x_conv.reshape(length, -1, HEADDIM), step_sizes, rates, bc_conv[:, :STATE], bc_conv[:, STATE:], segment, skip_gains)
    return mixed * jax.nn.silu(z_part)

def mamba_layer(residual, segment, gain_in, inner_w, shared_w, conv_w, conv_b, dt_shift, rate_logs, skip_gains, gain_mix, out_w):
    inv_in = lax.rsqrt(lax.optimization_barrier(jnp.mean(residual * residual, axis=1, keepdims=True)) + epsilon)
    normed = low(residual * inv_in * gain_in[None, :])
    inner_out = low_back(jnp.dot(normed, inner_w.reshape(D, 2 * INNER), precision=precise, preferred_element_type=jnp.float32)).reshape(-1, 2, INNER)
    shared_out = low_back(jnp.dot(normed, shared_w, precision=precise, preferred_element_type=jnp.float32))
    mix_pre = jax.checkpoint(mixer_sequence)(inner_out[:, 0], inner_out[:, 1], shared_out[:, :2 * STATE], shared_out[:, 2 * STATE:], conv_w[:, :INNER], conv_b[:INNER], conv_w[:, INNER:], conv_b[INNER:], dt_shift, rate_logs, skip_gains, segment)
    inv_mix = lax.rsqrt(lax.optimization_barrier(jnp.mean(mix_pre * mix_pre, axis=1, keepdims=True)) + epsilon)
    gated = low(mix_pre * inv_mix * gain_mix[None, :])
    branch = low_back(jnp.dot(gated, out_w, precision=precise, preferred_element_type=jnp.float32))
    return residual + branch

def two_layers(residual, segment, weight_values):
    gains_in, inner_all, shared_all, conv_w_all, conv_b_all, shift_all, rate_all, skip_all, mix_all, out_all = weight_values
    for layer_pos in range(LAYERS):
        residual = mamba_layer(residual, segment, gains_in[layer_pos], inner_all[layer_pos], shared_all[layer_pos], conv_w_all[layer_pos], conv_b_all[layer_pos], shift_all[layer_pos], rate_all[layer_pos], skip_all[layer_pos], mix_all[layer_pos], out_all[layer_pos])
    return residual

def reference(resid_in, segments, cotangent, norm_gain, inner_proj, shared_proj, conv_weight, conv_bias, dt_offset, rate_log, skip_gain, mix_gain, out_proj):
    weights = (norm_gain.astype(jnp.float32), inner_proj.astype(jnp.float32), shared_proj.astype(jnp.float32), conv_weight.astype(jnp.float32), conv_bias.astype(jnp.float32), dt_offset.astype(jnp.float32), rate_log.astype(jnp.float32), skip_gain.astype(jnp.float32), mix_gain.astype(jnp.float32), out_proj.astype(jnp.float32))
    groups = TOKENS // SEQ_LEN
    resid_groups = resid_in.reshape(groups, SEQ_LEN, D)
    seg_groups = segments.reshape(groups, SEQ_LEN)
    cot_groups = cotangent.reshape(groups, SEQ_LEN, D)

    def one_group(accum, pieces):
        resid_part, segment_part, cot_part = pieces

        def forward(resid_value, weight_values):
            return two_layers(resid_value, segment_part, weight_values)
        output, pullback = jax.vjp(forward, resid_part, weights)
        grad_resid, grad_weights = pullback(cot_part)
        accum = jax.tree.map(lambda running, addend: running + addend, accum, grad_weights)
        return (accum, (output, grad_resid))
    zeros = jax.tree.map(jnp.zeros_like, weights)
    totals, outcome = lax.scan(one_group, zeros, (resid_groups, seg_groups, cot_groups))
    outputs, grad_inputs = outcome
    return (outputs.reshape(TOKENS, D), grad_inputs.reshape(TOKENS, D), totals[0], totals[1], totals[2], totals[3], totals[4], totals[5], totals[6], totals[7], totals[8], totals[9])
```

```python
import jax
import jax.numpy as jnp
from jax import lax
from jax.experimental import pallas as pl
from jax.experimental.pallas import tpu as pltpu
from jax.sharding import PartitionSpec as P

D = 1024
HEADS = 32
HEADDIM = 64
STATE = 128
KCONV = 4
INNER = 2048
LANES = 128
ROWS = 128
SIDE = 3 * LANES

epsilon = 1e-05
precise = lax.Precision.HIGHEST
f32 = jnp.float32
bf16 = jnp.bfloat16


def dot(a, b, ca=1, cb=0, precision=None):
    return lax.dot_general(
        a, b, (((ca,), (cb,)), ((), ())), precision=precision, preferred_element_type=f32
    )


def sigmoid(a):
    return 1.0 / (1.0 + jnp.exp(-a))


def conv_rows(values, cols, weights):
    total = weights[4:5] + weights[3:4] * values
    for lag in range(1, KCONV):
        total = total + weights[3 - lag : 4 - lag] * (
            pltpu.roll(values, lag, 0) * cols[:, lag - 1 : lag]
        )
    return total


def conv_rows_back(gconv, values, cols, weights):
    length = values.shape[0]
    back = weights[3:4] * gconv
    taps = [None] * KCONV
    taps[3] = jnp.sum(gconv * values, axis=0, keepdims=True)
    for lag in range(1, KCONV):
        kept = gconv * cols[:, lag - 1 : lag]
        back = back + weights[3 - lag : 4 - lag] * pltpu.roll(kept, length - lag, 0)
        taps[3 - lag] = jnp.sum(kept * pltpu.roll(values, lag, 0), axis=0, keepdims=True)
    return back, taps + [jnp.sum(gconv, axis=0, keepdims=True)]


def iotas(shape):
    return lax.broadcasted_iota(jnp.int32, shape, 0), lax.broadcasted_iota(jnp.int32, shape, 1)


def row_blocks(length):
    return [(start, start + ROWS) for start in range(0, length, ROWS)]


def running_sum(values):
    row, col = iotas((ROWS, ROWS))
    lower = (row >= col).astype(f32)
    carry, parts = jnp.zeros((1, values.shape[1]), f32), []
    for start, stop in row_blocks(values.shape[0]):
        parts.append(dot(lower, values[start:stop], precision=precise) + carry)
        carry = parts[-1][ROWS - 1 : ROWS]
    return jnp.concatenate(parts, axis=0)


def running_sum_back(values):
    row, col = iotas((ROWS, ROWS))
    upper = (row <= col).astype(f32)
    carry, parts = jnp.zeros((1, values.shape[1]), f32), []
    for start, stop in reversed(row_blocks(values.shape[0])):
        parts.append(dot(upper, values[start:stop], precision=precise) + carry)
        carry = parts[-1][0:1]
    return jnp.concatenate(parts[::-1], axis=0)


def linked_later(cols_ref, segrow_ref, start, stop):
    row, col = iotas((stop - start, segrow_ref.shape[1] - start))
    return (row <= col) & (cols_ref[start:stop, 3:4] == segrow_ref[0:1, start:])


def step_sizes_of(shared_ref, heads_ref):
    pre = shared_ref[:, 2 * STATE :] + heads_ref[0:1]
    return pre, jnp.maximum(pre, 0.0) + jnp.log1p(jnp.exp(-jnp.abs(pre)))


def column_of(array, head):
    lane = lax.broadcasted_iota(jnp.int32, array.shape, 1)
    return jnp.sum(jnp.where(lane == head, array, 0.0), axis=1, keepdims=True)


def forward_kernel(
    z_ref, x_ref, shared_ref, cols_ref, segrow_ref, chan_ref, side_ref, heads_ref,
    y_ref, mix_ref,
    pair_ref, b_ref, c_ref, dt_ref, cum_ref, cumt_ref,
):
    step = pl.program_id(0)
    length = z_ref.shape[0]
    kept = pairs_kept(length)

    def pairs(start, stop):
        row, col = iotas((ROWS, stop))
        linked = (row + start >= col) & (cols_ref[start:stop, 3:4] == segrow_ref[0:1, :stop])
        return jnp.where(linked, dot(c_ref[start:stop], b_ref[:stop], 1, 1), 0.0)

    @pl.when(step == 0)
    def _():
        conv = conv_rows(shared_ref[:, : 2 * STATE], cols_ref[...], side_ref[...])
        bc = (conv * sigmoid(conv)).astype(bf16)
        b_ref[...] = bc[:, :STATE]
        c_ref[...] = bc[:, STATE:]
        for start, stop in row_blocks(length) if kept else []:
            pair_ref[start:stop, :stop] = pairs(start, stop)
        dt = step_sizes_of(shared_ref, heads_ref)[1]
        dt_ref[...] = dt
        cum = running_sum(-dt * heads_ref[1:2])
        cum_ref[...] = cum
        cumt_ref[...] = cum.T

    conv = conv_rows(x_ref[...], cols_ref[...], chan_ref[...])
    xs = conv * sigmoid(conv)
    z = z_ref[...]
    halves = []
    for half in range(LANES // HEADDIM):
        head = step * (LANES // HEADDIM) + half
        cumcol = column_of(cum_ref[...], head)
        cumrow = cumt_ref[pl.ds(head, 1), :]
        xdt = xs[:, half * HEADDIM : (half + 1) * HEADDIM] * column_of(dt_ref[...], head)
        xdt = xdt.astype(bf16)
        parts = []
        for start, stop in row_blocks(length):
            decay = jnp.exp(jnp.minimum(cumcol[start:stop] - cumrow[:, :stop], 0.0))
            pair = pair_ref[start:stop, :stop] if kept else pairs(start, stop)
            mixing = (pair * decay).astype(bf16)
            parts.append(dot(mixing, xdt[:stop]))
        halves.append(jnp.concatenate(parts, axis=0))
    y = jnp.concatenate(halves, axis=1) + chan_ref[6:7] * xs
    y_ref[...] = y
    mix_ref[...] = y * (z * sigmoid(z))


def backward_kernel(
    z_ref, x_ref, y_ref, gg_ref, shared_ref, cols_ref, segrow_ref, chan_ref, side_ref, heads_ref,
    gz_ref, gx_ref, gshared_ref, gchan_ref, gside_ref, gheads_ref,
    pair_ref, gpair_ref, gb_ref, gc_ref, b_ref, c_ref, dt_ref, cum_ref, cumt_ref, du_ref, mrow_ref,
):
    step = pl.program_id(0)
    length = z_ref.shape[0]
    kept = pairs_kept(length)

    def pairs(start, stop):
        linked = linked_later(cols_ref, segrow_ref, start, stop)
        return jnp.where(linked, dot(b_ref[start:stop], c_ref[start:], 1, 1), 0.0)

    def add_pair_grad(start, stop, gpair):
        linked = linked_later(cols_ref, segrow_ref, start, stop)
        gpair = jnp.where(linked, gpair, 0.0)
        gb_ref[start:stop] += dot(gpair.astype(bf16), c_ref[start:])
        gc_ref[start:] += dot(gpair.T.astype(bf16), b_ref[start:stop])

    @pl.when(step == 0)
    def _():
        conv = conv_rows(shared_ref[:, : 2 * STATE], cols_ref[...], side_ref[...])
        bc = (conv * sigmoid(conv)).astype(bf16)
        b_ref[...] = bc[:, :STATE]
        c_ref[...] = bc[:, STATE:]
        for start, stop in row_blocks(length) if kept else []:
            pair_ref[start:stop, start:] = pairs(start, stop)
            gpair_ref[start:stop, start:] = jnp.zeros((ROWS, length - start), f32)
        gb_ref[...] = jnp.zeros_like(gb_ref)
        gc_ref[...] = jnp.zeros_like(gc_ref)
        dt = step_sizes_of(shared_ref, heads_ref)[1]
        dt_ref[...] = dt
        cum = running_sum(-dt * heads_ref[1:2])
        cum_ref[...] = cum
        cumt_ref[...] = cum.T
        du_ref[...] = jnp.zeros_like(du_ref)
        mrow_ref[...] = jnp.zeros_like(mrow_ref)

    cols = cols_ref[...]
    x_raw = x_ref[...]
    conv = conv_rows(x_raw, cols, chan_ref[...])
    gate = sigmoid(conv)
    xs = conv * gate
    z = z_ref[...]
    zgate = sigmoid(z)
    zsilu = z * zgate
    y = y_ref[...]
    mix = y * zsilu
    gg = gg_ref[...]
    ggi = gg * cols[:, 4:5]
    gmix = ggi * chan_ref[5:6] - mix * cols[:, 5:6]
    ggain = jnp.sum(ggi * mix, axis=0, keepdims=True)
    gz_ref[...] = (gmix * y * (zgate * (1.0 + z * (1.0 - zgate)))).astype(bf16)
    gy = gmix * zsilu
    gskip = jnp.sum(xs * gy, axis=0, keepdims=True)
    xs_low, gy_low = xs.astype(bf16), gy.astype(bf16)
    halves = []
    for half in range(LANES // HEADDIM):
        head = step * (LANES // HEADDIM) + half
        span = slice(half * HEADDIM, (half + 1) * HEADDIM)
        cumcol = column_of(cum_ref[...], head)
        dtcol = column_of(dt_ref[...], head)
        cumrow = cumt_ref[pl.ds(head, 1), :]
        xh, gh = xs_low[:, span], gy_low[:, span]
        parts, dus = [], []
        mrow = jnp.zeros((1, length), f32)
        for start, stop in row_blocks(length):
            pair = pair_ref[start:stop, start:] if kept else pairs(start, stop)
            decay = jnp.exp(jnp.minimum(cumrow[:, start:] - cumcol[start:stop], 0.0))
            ga = decay * dot(xh[start:stop], gh[start:], 1, 1)
            u = pair * ga
            dtb = dtcol[start:stop]
            parts.append(dot((pair * decay).astype(bf16), gh[start:]) * dtb)
            if kept:
                gpair_ref[start:stop, start:] += ga * dtb
            else:
                add_pair_grad(start, stop, ga * dtb)
            dus.append(jnp.sum(u, axis=1, keepdims=True))
            sums = jnp.sum(u * dtb, axis=0, keepdims=True)
            if start:
                sums = jnp.concatenate([jnp.zeros((1, start), f32), sums], axis=1)
            mrow = mrow + sums
        halves.append(jnp.concatenate(parts, axis=0))
        mrow_ref[pl.ds(head, 1), :] = mrow
        lane = lax.broadcasted_iota(jnp.int32, du_ref.shape, 1)
        du_ref[...] = jnp.where(lane == head, jnp.concatenate(dus, axis=0), du_ref[...])
    gxs = jnp.concatenate(halves, axis=1) + chan_ref[6:7] * gy
    gconv = gxs * (gate * (1.0 + conv * (1.0 - gate)))
    gx, grows = conv_rows_back(gconv, x_raw, cols, chan_ref[...])
    gx_ref[...] = gx.astype(bf16)
    for place, value in enumerate(grows + [ggain, gskip]):
        gchan_ref[place : place + 1, :] = value
    gchan_ref[7:8, :] = jnp.zeros((1, LANES), f32)

    @pl.when(step == pl.num_programs(0) - 1)
    def _():
        for start, stop in row_blocks(length) if kept else []:
            add_pair_grad(start, stop, gpair_ref[start:stop, start:])
        raw = shared_ref[:, : 2 * STATE]
        conv = conv_rows(raw, cols_ref[...], side_ref[...])
        gate = sigmoid(conv)
        gconv = jnp.concatenate([gb_ref[...], gc_ref[...]], axis=1) * (gate * (1.0 + conv * (1.0 - gate)))
        graw, rows = conv_rows_back(gconv, raw, cols_ref[...], side_ref[...])
        gshared_ref[:, : 2 * STATE] = graw.astype(bf16)
        for place, value in enumerate(rows):
            gside_ref[place : place + 1, :] = value
        gside_ref[5:8, :] = jnp.zeros((3, 2 * STATE), f32)
        pre, dt = step_sizes_of(shared_ref, heads_ref)
        rate = heads_ref[1:2]
        du = du_ref[...]
        gcum = mrow_ref[...].T - du * dt
        later = running_sum_back(gcum)
        gdt = (du - rate * later) * sigmoid(pre)
        gshared_ref[:, 2 * STATE :] = gdt.astype(bf16)
        gheads_ref[0:1, :] = jnp.sum(gdt, axis=0, keepdims=True)
        gheads_ref[1:2, :] = -rate * jnp.sum(dt * later, axis=0, keepdims=True)
        gheads_ref[2:8, :] = jnp.zeros((6, LANES), f32)


def whole(shape):
    return pl.BlockSpec(shape, lambda i: (0, 0))


def lanes_block(rows, shift=0):
    return pl.BlockSpec((rows, LANES), lambda i: (0, i + shift))


def pairs_kept(length):
    return length <= 1024


def params():
    return pltpu.CompilerParams(
        vmem_limit_bytes=60 * 1024 * 1024, dimension_semantics=("arbitrary",)
    )


def mixer_forward(inner_out, shared_out, cols, segrow, chan, side, heads):
    length, width = inner_out.shape[0], inner_out.shape[1] // 2
    steps = width // LANES
    square = length if pairs_kept(length) else LANES
    return pl.pallas_call(
        forward_kernel,
        grid=(steps,),
        in_specs=[
            lanes_block(length), lanes_block(length, steps), whole((length, SIDE)),
            whole(cols.shape), whole(segrow.shape), lanes_block(8),
            whole(side.shape), whole(heads.shape),
        ],
        out_specs=[lanes_block(length)] * 2,
        out_shape=[jax.ShapeDtypeStruct((length, width), f32)] * 2,
        scratch_shapes=[
            pltpu.VMEM((square, square), f32),
            pltpu.VMEM((length, STATE), bf16),
            pltpu.VMEM((length, STATE), bf16),
            pltpu.VMEM((length, LANES), f32),
            pltpu.VMEM((length, LANES), f32),
            pltpu.VMEM((LANES, length), f32),
        ],
        compiler_params=params(),
        name="mixer_forward",
    )(inner_out, inner_out, shared_out, cols, segrow, chan, side, heads)


def mixer_backward(inner_out, y, grad_gated, shared_out, cols, segrow, chan, side, heads):
    length, width = y.shape
    steps = width // LANES
    square = length if pairs_kept(length) else LANES
    return pl.pallas_call(
        backward_kernel,
        grid=(steps,),
        in_specs=[
            lanes_block(length), lanes_block(length, steps), lanes_block(length),
            lanes_block(length), whole((length, SIDE)), whole(cols.shape),
            whole(segrow.shape), lanes_block(8), whole(side.shape), whole(heads.shape),
        ],
        out_specs=[
            lanes_block(length), lanes_block(length), whole((length, SIDE)),
            lanes_block(8), whole((8, 2 * STATE)), whole((8, LANES)),
        ],
        out_shape=[
            jax.ShapeDtypeStruct((length, width), bf16),
            jax.ShapeDtypeStruct((length, width), bf16),
            jax.ShapeDtypeStruct((length, SIDE), bf16),
            jax.ShapeDtypeStruct((8, width), f32),
            jax.ShapeDtypeStruct((8, 2 * STATE), f32),
            jax.ShapeDtypeStruct((8, LANES), f32),
        ],
        scratch_shapes=[
            pltpu.VMEM((square, square), f32),
            pltpu.VMEM((square, square), f32),
            pltpu.VMEM((length, STATE), f32),
            pltpu.VMEM((length, STATE), f32),
            pltpu.VMEM((length, STATE), bf16),
            pltpu.VMEM((length, STATE), bf16),
            pltpu.VMEM((length, LANES), f32),
            pltpu.VMEM((length, LANES), f32),
            pltpu.VMEM((LANES, length), f32),
            pltpu.VMEM((length, LANES), f32),
            pltpu.VMEM((LANES, length), f32),
        ],
        compiler_params=params(),
        name="mixer_backward",
    )(inner_out, inner_out, y, grad_gated, shared_out, cols, segrow, chan, side, heads)


def on_device(
    resid_in, segments, cotangent, norm_gain, inner_proj, shared_proj, conv_weight, conv_bias,
    dt_offset, rate_log, skip_gain, mix_gain, out_proj,
):
    side_index = lax.axis_index("tensor")
    sides_count = HEADS // (inner_proj.shape[3] // HEADDIM)
    paired = sides_count == 2
    first = side_index == 0
    width = inner_proj.shape[3]
    heads = width // HEADDIM
    length = segments.shape[0]
    rows = length // sides_count
    layers = norm_gain.shape[0]
    chan_start = side_index * width
    head_start = side_index * heads

    def swap(value):
        return lax.ppermute(value, "tensor", [(0, 1), (1, 0)])

    def gather_sides(mine):
        if not paired:
            return lax.all_gather(mine, "tensor", axis=0)
        other = swap(mine)
        return jnp.stack([jnp.where(first, mine, other), jnp.where(first, other, mine)], axis=0)

    def gather_rows(mine):
        return gather_sides(mine).reshape(-1, mine.shape[1])

    def side_sum_of(mine):
        return mine + swap(mine) if paired else lax.psum(mine, "tensor")

    def scatter_sum(part):
        if not paired:
            return lax.psum_scatter(part, "tensor", scatter_dimension=0, tiled=True)
        other = lax.dynamic_slice_in_dim(part, (1 - side_index) * rows, rows, 0)
        mine = lax.dynamic_slice_in_dim(part, side_index * rows, rows, 0)
        return mine + swap(other.astype(bf16)).astype(f32)

    def cut(values, start, size):
        return lax.dynamic_slice_in_dim(values, start, size, values.ndim - 1)

    position = lax.iota(jnp.int32, length)
    columns = []
    for lag in range(1, KCONV):
        columns.append(((jnp.roll(segments, lag) == segments) & (position >= lag)).astype(f32))
    seg_float = segments.astype(f32)
    columns.append(seg_float)
    segrow = jnp.broadcast_to(seg_float[None, :], (8, length))

    def cols_with(inv, coef):
        zero = jnp.zeros((length,), f32)
        return jnp.stack(columns + [inv, coef, zero, zero], axis=1)

    zero = jnp.zeros((length,), f32)
    plain_cols = cols_with(zero, zero)

    inner_ws, out_ws, side_ws, chans, sides, head_rows = [], [], [], [], [], []
    for layer in range(layers):
        inner_ws.append(
            lax.all_gather(inner_proj[layer].reshape(-1, 2 * width), "dp", axis=0, tiled=True)
        )
        out_ws.append(lax.all_gather(out_proj[layer].T, "dp", axis=0, tiled=True))
        shared_w = shared_proj[layer]
        side_ws.append(
            jnp.concatenate(
                [
                    shared_w[:, : 2 * STATE],
                    cut(shared_w, 2 * STATE + head_start, heads),
                    jnp.zeros((D, LANES - heads), bf16),
                ],
                axis=1,
            )
        )
        chans.append(
            jnp.concatenate(
                [
                    cut(conv_weight[layer], chan_start, width),
                    cut(conv_bias[layer], chan_start, width)[None],
                    cut(mix_gain[layer], chan_start, width)[None],
                    jnp.repeat(cut(skip_gain[layer], head_start, heads), HEADDIM)[None],
                    jnp.zeros((1, width), f32),
                ],
                axis=0,
            )
        )
        sides.append(
            jnp.concatenate(
                [
                    conv_weight[layer][:, INNER:],
                    conv_bias[layer][None, INNER:],
                    jnp.zeros((3, 2 * STATE), f32),
                ],
                axis=0,
            )
        )
        head_rows.append(
            jnp.zeros((8, LANES), f32)
            .at[0, :heads].set(cut(dt_offset[layer], head_start, heads))
            .at[1, :heads].set(jnp.exp(cut(rate_log[layer], head_start, heads)))
        )

    stored = []
    residual = resid_in
    for layer in range(layers):
        gain_in = norm_gain[layer]
        inv_in = lax.rsqrt(jnp.mean(residual * residual, axis=1) + epsilon)
        normed = (residual * inv_in[:, None] * gain_in[None, :]).astype(bf16)
        normed_all = gather_rows(normed)
        shared_out = dot(normed_all, side_ws[layer])
        inner_out = dot(normed_all, inner_ws[layer])
        y, mix_pre = mixer_forward(
            inner_out, shared_out, plain_cols, segrow, chans[layer], sides[layer],
            head_rows[layer],
        )
        squares = jnp.sum(mix_pre * mix_pre, axis=1)
        squares = side_sum_of(squares)
        inv_mix = lax.rsqrt(squares / INNER + epsilon)
        gated = (mix_pre * inv_mix[:, None] * chans[layer][5:6]).astype(bf16)
        stored.append((residual, inv_in, normed_all, shared_out, inner_out, y, mix_pre, inv_mix, gated))
        residual = residual + scatter_sum(dot(gated, out_ws[layer], 1, 1))
    layer_output = residual

    grad_resid = cotangent
    results = [None] * layers
    for layer in reversed(range(layers)):
        residual, inv_in, normed_all, shared_out, inner_out, y, mix_pre, inv_mix, gated = stored[layer]
        grad_all = gather_rows(grad_resid.astype(bf16))
        grad_gated = dot(grad_all, out_ws[layer])
        grad_out = dot(grad_all, gated, 0, 0).astype(bf16)
        out_shard = lax.psum_scatter(grad_out, "dp", scatter_dimension=0, tiled=True)
        inner_dot = jnp.sum(grad_gated * chans[layer][5:6] * mix_pre, axis=1)
        inner_dot = side_sum_of(inner_dot)
        coef = inv_mix * inv_mix * inv_mix * inner_dot / INNER
        gz, gx, gshared, gchan, gside, gheads = mixer_backward(
            inner_out, y, grad_gated, shared_out, cols_with(inv_mix, coef), segrow,
            chans[layer], sides[layer], head_rows[layer],
        )
        part = (
            dot(gz, inner_ws[layer][:, :width], 1, 1)
            + dot(gx, inner_ws[layer][:, width:], 1, 1)
            + dot(gshared, side_ws[layer], 1, 1)
        )
        grad_normed = scatter_sum(part)
        grad_side = dot(normed_all, gshared, 0, 0)
        gain_in = norm_gain[layer]
        weighted = grad_normed * gain_in[None, :]
        grad_gain_in = jnp.sum(grad_normed * residual * inv_in[:, None], axis=0)
        input_dot = jnp.sum(weighted * residual, axis=1)
        cubed = inv_in * inv_in * inv_in
        grad_resid = (
            grad_resid + weighted * inv_in[:, None] - residual * (cubed * input_dot / D)[:, None]
        )
        gskip = jnp.sum(gchan[6].reshape(heads, HEADDIM), axis=1)
        small = jnp.concatenate(
            [
                gchan[:6].reshape(-1), gheads[0, :heads], gheads[1, :heads], gskip,
                gside[:5].reshape(-1), grad_gain_in,
            ]
        )
        small_rows = 128 * (-(-small.shape[0] // (128 * SIDE)))
        small = jnp.pad(small, (0, small_rows * SIDE - small.shape[0])).reshape(small_rows, SIDE)
        packed = jnp.concatenate([grad_side, small], axis=0).astype(bf16)
        packed = lax.psum_scatter(packed, "dp", scatter_dimension=0, tiled=True)
        packed = lax.all_gather(packed, "dp", axis=0, tiled=True)
        packed = gather_sides(packed).astype(f32)
        inner_shard = lax.psum_scatter(
            jnp.concatenate([dot(normed_all, gz, 0, 0), dot(normed_all, gx, 0, 0)], axis=1).astype(bf16),
            "dp", scatter_dimension=0, tiled=True,
        )
        summed = jnp.sum(packed, axis=0)
        grad_dt = packed[:, :D, 2 * STATE : 2 * STATE + heads]
        grad_dt = jnp.transpose(grad_dt, (1, 0, 2)).reshape(D, HEADS)
        grad_shared = jnp.concatenate([summed[:D, : 2 * STATE], grad_dt], axis=1)
        flat = packed[:, D:].reshape(sides_count, -1)
        flat_sum = summed[D:].reshape(-1)

        def channels(place):
            return flat[:, place * width : (place + 1) * width].reshape(-1)

        def of_heads(place):
            start = 6 * width + place * heads
            return flat[:, start : start + heads].reshape(-1)

        base = 6 * width + 3 * heads
        side_sum = flat_sum[base : base + 10 * STATE].reshape(5, 2 * STATE)
        conv_x = jnp.stack([channels(k) for k in range(KCONV)], axis=0)
        results[layer] = (
            flat_sum[base + 10 * STATE : base + 10 * STATE + D],
            inner_shard.astype(f32).reshape(-1, 2, width),
            grad_shared,
            jnp.concatenate([conv_x, side_sum[:4]], axis=1),
            jnp.concatenate([channels(4), side_sum[4]], axis=0),
            of_heads(0),
            of_heads(1),
            of_heads(2),
            channels(5),
            out_shard.T.astype(f32),
        )
    stacked = [
        jnp.stack([results[layer][member] for layer in range(layers)], axis=0)
        for member in range(10)
    ]
    return (layer_output, grad_resid, *stacked)


def solution(mesh):
    tokens = P(("dp", "tensor"), None)
    weights = (P(None, "dp", None, "tensor"), P(None, "tensor", "dp"))
    in_specs = (
        tokens, P("dp"), tokens, P(), weights[0], P(), P(), P(), P(), P(), P(), P(), weights[1],
    )
    out_specs = (
        tokens, tokens, P(), weights[0], P(), P(), P(), P(), P(), P(), P(), weights[1],
    )
    return jax.shard_map(
        on_device, mesh=mesh, in_specs=in_specs, out_specs=out_specs, check_vma=False
    )
```
